512 devices in a mesh: layer: 8 (over z_lo), row: 8 (over z_hi, x), col: 8 (over y, core).
Axes of the slice: x: 4, y: 4, z: 16 (z_hi: 2, z_lo: 8; z = z_hi * 8 + z_lo), core: 2. Of those that a mesh axis runs over, the one named last changes fastest.
Arguments:
- tensor: bfloat16 [512, 128, 8192], P(('layer', 'row'), None, 'col'), may hold values from -6 to 6
- coefs: bfloat16 [8192, 384], P(('col', 'layer')), may hold values from -0.0625 to 0.0625
- tile_mask: int32 [8, 8, 128], replicated, may hold values from 0 to 1, as said below
- coef_mask: int32 [128, 6], replicated, may hold values 0 or 1
- batch_start: int32 [1], replicated, may hold values from 0 to 128
Outputs:
- half_transformed: bfloat16 [512, 128, 256], P(('layer', 'row'), 'col')
The draws below stay inside these ranges and needn't reach their ends.
Inputs may be any that keep to these rules, and one draw needn't show every extreme that they name: `tile_mask`: 1 where the tile is stored as nonzero, else 0. `coef_mask`: 1 where the coefficient tile is read, else 0. The batch is the columns batch_start to batch_start + 255 of coefs.
All inputs are finite; a program needn't handle non-finite values.
Results may differ from the reference program's by a relative error of at most 0.00155.
Values may be sent and summed in bfloat16 or wider, within the bound.
No kernel may reach another device: no remote copies, remote signals or barrier semaphores. Data moves between devices by JAX's collectives and lax.ppermute only.
A program may use at most 64 MiB of HBM per device.

```python
import jax
import jax.numpy as jnp
from jax import lax

TILE = 64
MU_DEV = 16
BATCH = 256
OCC_WIN = 384
AUX = 512
MU = 128
NU = 8192


def draw_tile_mask(key, part):
    key = jax.random.fold_in(key, 11)
    level_key, cell_key = jax.random.split(key)
    levels = jax.random.randint(level_key, (AUX // TILE, 1, 1), 1, 5)
    cells = jax.random.randint(cell_key, (AUX // TILE, MU // MU_DEV, NU // TILE), 0, 4)
    return (cells < levels).astype(jnp.int32)


def with_ends(array, rng, low, largest):
    longest = array.shape.index(max(array.shape))
    spots = []
    for shift in (0, 1):
        where = [jax.random.randint(jax.random.fold_in(rng, axis), (), 0, length) for axis, length in enumerate(array.shape)]
        where[longest] = (where[longest] + shift) % array.shape[longest]
        spots.append(tuple(where))
    return array.at[spots[0]].set(low).at[spots[1]].set(largest)


def shard_levels(rng, extent, shards, least, top_value):
    factor_of, own = 1.0, jax.random.fold_in(rng, 6)
    for dim, parts in shards:
        steps = jnp.exp(jax.random.uniform(jax.random.fold_in(own, dim), (parts,), jnp.float32, least / len(shards), top_value / len(shards)))
        factor_of = factor_of * jnp.repeat(steps, extent[dim] // parts).reshape([-1 if axis == dim else 1 for axis in range(len(extent))])
    return factor_of


def noise(rng, extent, deviation, limit, cuts=(), kind=jnp.bfloat16):
    entries = jax.random.normal(rng, extent, jnp.float32) * deviation
    if len(cuts) > 0:
        entries = shard_levels(rng, extent, cuts, -0.22, 0.18) * entries
    return jnp.clip(entries, min=-limit, max=limit).astype(kind)


def setup_inputs(seed: int = 0) -> dict:
    keys = jax.random.split(jax.random.key(seed), 6)
    return {
        "tensor": noise(keys[0], (AUX, MU, NU), 1.0, 6.0, ((0, 64), (2, 8))),
        "coefs": noise(keys[1], (NU, OCC_WIN), NU ** -0.5, 0.0625, ((0, 64),)),
        "tile_mask": draw_tile_mask(jax.random.fold_in(keys[5], 71), 0),
        "coef_mask": with_ends((jax.random.randint(keys[3], (NU // TILE, OCC_WIN // TILE), 0, 4) < 3).astype(jnp.int32), jax.random.fold_in(keys[3], 1), 0, 1),
        "batch_start": jax.random.randint(keys[4], (1,), 0, 2 * TILE + 1).astype(jnp.int32),
    }


def expand(tile_table, inner_rows, inner_cols):
    shape_rows = tile_table.shape[0]
    shape_cols = tile_table.shape[1]
    spread = jnp.broadcast_to(tile_table[:, None, :, None], (shape_rows, inner_rows, shape_cols, inner_cols))
    return spread.reshape(shape_rows * inner_rows, shape_cols * inner_cols)


def reference(tensor, coefs, tile_mask, coef_mask, batch_start):
    coef_keep = expand(coef_mask, TILE, TILE)
    masked_coefs = jnp.where(coef_keep > 0, coefs, jnp.zeros_like(coefs))
    batch_coefs = lax.dynamic_slice_in_dim(masked_coefs, batch_start[0].astype(jnp.int32), BATCH, 1)
    aux_tiles = tensor.reshape(AUX // TILE, TILE, MU, NU)

    def contract_tile(operands):
        aux_block, tile_table = operands
        keep_mask = expand(tile_table, MU_DEV, TILE)
        masked = jnp.where(keep_mask[None] > 0, aux_block, jnp.zeros_like(aux_block))
        product = jnp.dot(masked.reshape(TILE * MU, NU), batch_coefs, preferred_element_type=jnp.float32)
        return product.reshape(TILE, MU, BATCH).astype(jnp.bfloat16)

    result = lax.map(contract_tile, (aux_tiles, tile_mask))
    return result.reshape(AUX, MU, BATCH)
```

```python
import functools

import jax
import jax.numpy as jnp
from jax import lax
from jax.experimental import pallas as pl
from jax.experimental.pallas import tpu as pltpu
from jax.sharding import Mesh, PartitionSpec as P

TILE = 64
BATCH = 256
LAYERS = 8
COLS = 8
EVEN_OFFSETS = (-3, -2, -1, 0)
ODD_OFFSETS = (1, 2, 3, 0)
SLOT_BLOCKS = EVEN_OFFSETS + tuple(1 + offset for offset in ODD_OFFSETS)


def fetch_pairs():
    pairs = []
    for z in range(16):
        for x in range(4):
            offset = (ODD_OFFSETS if z % 2 else EVEN_OFFSETS)[x]
            source = (z + offset) % 16
            place = lambda at: (at % 8) * 8 + (at // 8) * 4 + x
            pairs.append((place(source), place(z)))
    return pairs


def coefs_kernel(scalars, mask_ref, coefs_ref, out_ref):
    first = scalars[0]
    start = scalars[1]
    rows, width = coefs_ref.shape
    lane_tile = lax.broadcasted_iota(jnp.int32, (1, width), 1) // TILE
    values = coefs_ref[...].astype(jnp.float32)
    parts = []
    for t in range(rows // TILE):
        keep = jnp.zeros((1, width), jnp.int32)
        for j in range(width // TILE):
            keep = jnp.where(lane_tile == j, mask_ref[j, first + t], keep)
        parts.append(jnp.where(keep > 0, values[t * TILE:(t + 1) * TILE], 0.0))
    kept = jnp.concatenate(parts, axis=0)
    turned = pltpu.roll(kept, lax.rem(width - start, width), 1)
    out_ref[...] = turned[:, :BATCH].astype(out_ref.dtype)


def masked_batch(coefs, coef_mask, scalars):
    return pl.pallas_call(
        coefs_kernel,
        out_shape=jax.ShapeDtypeStruct((coefs.shape[0], BATCH), jnp.bfloat16),
        in_specs=[
            pl.BlockSpec(memory_space=pltpu.SMEM),
            pl.BlockSpec(memory_space=pltpu.SMEM),
            pl.BlockSpec(memory_space=pltpu.VMEM),
        ],
        out_specs=pl.BlockSpec(memory_space=pltpu.VMEM),
        name="masked_batch",
    )(scalars, coef_mask.T, coefs)


def mask_kernel(scalars, mask_ref, tensor_ref, out_ref):
    block = scalars[pl.program_id(0)]
    first = scalars[LAYERS + 1] * 16 + 2 * block
    left = lax.broadcasted_iota(jnp.int32, (1, 1, 128), 2) < TILE
    mu_dev = tensor_ref.shape[1] // COLS
    for c in range(COLS):
        keep = jnp.where(left, mask_ref[0, c, first], mask_ref[0, c, first + 1])
        part = tensor_ref[:, c * mu_dev:(c + 1) * mu_dev, :]
        out_ref[c] = jnp.where(keep > 0, part, jnp.zeros_like(part))


def masked_tensor(tensor, tile_mask, scalars):
    aux, mu, nu = tensor.shape
    return pl.pallas_call(
        mask_kernel,
        out_shape=jax.ShapeDtypeStruct((COLS, aux, mu // COLS, nu), jnp.bfloat16),
        grid_spec=pltpu.PrefetchScalarGridSpec(
            num_scalar_prefetch=1,
            grid=(LAYERS,),
            in_specs=[
                pl.BlockSpec((1, 8, 128), lambda s, sc: (sc[LAYERS], 0, 0), memory_space=pltpu.SMEM),
                pl.BlockSpec((aux, mu, 128), lambda s, sc: (0, 0, sc[s])),
            ],
            out_specs=pl.BlockSpec((COLS, aux, mu // COLS, 128), lambda s, sc: (0, 0, 0, s)),
        ),
        name="masked_tensor",
        cost_estimate=pl.CostEstimate(flops=2 * tensor.size, bytes_accessed=4 * tensor.size, transcendentals=0),
    )(scalars, tile_mask, tensor)


def on_device(tensor, coefs, tile_mask, coef_mask, batch_start):
    lp, lb = lax.axis_index("lp"), lax.axis_index("lb")
    layer = 2 * lp + lb
    col = lax.axis_index("col")
    aux_dev, mu_all, nu_col = tensor.shape
    mine = masked_batch(coefs, coef_mask, jnp.stack([(col * LAYERS + layer) * 2, batch_start[0]]))
    fetched = lax.ppermute(mine, ("lp", "lb", "zh", "x"), fetch_pairs())
    spread = lax.all_to_all(jnp.broadcast_to(fetched[None], (LAYERS, *fetched.shape)), ("lb", "x"), 0, 0, tiled=True)
    slots = [lax.rem(2 * lp + (8 + offset), LAYERS) for offset in SLOT_BLOCKS]
    masked = masked_tensor(tensor, tile_mask, jnp.stack([*slots, layer, col]))
    partial = jnp.dot(masked.reshape(aux_dev * mu_all, nu_col), spread.reshape(nu_col, BATCH), preferred_element_type=jnp.float32)
    got = lax.all_to_all(partial.reshape(COLS, aux_dev * mu_all // COLS, BATCH), "col", 0, 0, tiled=True)
    return jnp.sum(got, axis=0).astype(jnp.bfloat16).reshape(aux_dev, mu_all // COLS, BATCH)


def solution(mesh):
    fine = Mesh(mesh.devices.reshape(4, 2, 2, 4, 8), ("lp", "lb", "zh", "x", "col"))
    aux = ("lp", "lb", "zh", "x")
    in_specs = (P(aux, None, "col"), P(("col", "lp", "lb"), None), P(), P(), P())
    out_specs = P(aux, "col", None)
    return jax.shard_map(on_device, mesh=fine, in_specs=in_specs, out_specs=out_specs, check_vma=False)
```

```python
import jax
import jax.numpy as jnp
from jax import lax
from jax.experimental import pallas as pl
from jax.experimental.pallas import tpu as pltpu
from jax.sharding import Mesh, PartitionSpec as P

TILE = 64
BATCH = 256
HALF = 128
LAYERS = 8
COLS = 8
SCALE_ROWS = 16
MIB = 1 << 20
EVEN_OFFSETS = (-3, -2, -1, 0)
ODD_OFFSETS = (1, 2, 3, 0)
SLOT_BLOCKS = EVEN_OFFSETS + tuple(1 + offset for offset in ODD_OFFSETS)


def fetch_pairs():
    pairs = []
    for z in range(16):
        for x in range(4):
            offset = (ODD_OFFSETS if z % 2 else EVEN_OFFSETS)[x]
            source = (z + offset) % 16
            pairs.append(((source % 8) * 8 + (source // 8) * 4 + x, (z % 8) * 8 + (z // 8) * 4 + x))
    return pairs


def pick(table, index):
    value = jnp.int32(table[0])
    for at in range(1, len(table)):
        value = jnp.where(index == at, jnp.int32(table[at]), value)
    return value


def spread_kernel(start_ref, mask_ref, coefs_ref, out_ref):
    rows, width = coefs_ref.shape
    slot = 4 * lax.axis_index("lb") + lax.axis_index("x")
    block = lax.rem(2 * lax.axis_index("lp") + LAYERS + pick(SLOT_BLOCKS, slot), LAYERS)
    first = (lax.axis_index("col") * LAYERS + block) * (rows // TILE)
    lane_tile = lax.broadcasted_iota(jnp.int32, (1, width), 1) // TILE
    turn = lax.rem(width - start_ref[0], width)
    for t in range(rows // TILE):
        keep = jnp.zeros((1, width), jnp.int32)
        for j in range(width // TILE):
            keep = jnp.where(lane_tile == j, mask_ref[j, first + t], keep)
        values = coefs_ref[t * TILE:(t + 1) * TILE, :].astype(jnp.float32)
        kept = jnp.where(keep > 0, values, 0.0)
        batch = pltpu.roll(kept, turn, 1)[:, :BATCH].astype(out_ref.dtype)
        for s in range(LAYERS):
            out_ref[s, t * TILE:(t + 1) * TILE, :] = batch


def spread_batch(fetched, coef_mask, batch_start):
    return pl.pallas_call(
        spread_kernel,
        out_shape=jax.ShapeDtypeStruct((LAYERS, fetched.shape[0], BATCH), jnp.bfloat16),
        in_specs=[
            pl.BlockSpec(memory_space=pltpu.SMEM),
            pl.BlockSpec(memory_space=pltpu.SMEM),
            pl.BlockSpec(memory_space=pltpu.VMEM),
        ],
        out_specs=pl.BlockSpec(memory_space=pltpu.VMEM),
        compiler_params=pltpu.CompilerParams(vmem_limit_bytes=4 * MIB),
        name="spread_batch",
    )(batch_start, coef_mask.T, fetched)


def mask_kernel(mask_ref, tensor_ref, out_ref):
    layer = 2 * lax.axis_index("lp") + lax.axis_index("lb")
    col = lax.axis_index("col")
    mu_dev = tensor_ref.shape[1] // COLS
    left = lax.broadcasted_iota(jnp.int32, (1, 1, HALF), 2) < TILE
    for s in range(LAYERS):
        block = lax.rem(2 * lax.axis_index("lp") + LAYERS + SLOT_BLOCKS[s], LAYERS)
        first = col * (2 * LAYERS) + 2 * block
        lanes = pl.ds(pl.multiple_of(block * HALF, HALF), HALF)
        for c in range(COLS):
            keep = jnp.where(left, mask_ref[layer, c, first], mask_ref[layer, c, first + 1])
            part = tensor_ref[:, c * mu_dev:(c + 1) * mu_dev, lanes]
            out_ref[c, :, :, s * HALF:(s + 1) * HALF] = jnp.where(keep > 0, part, jnp.zeros_like(part))


def masked_tensor(tensor, tile_mask):
    aux, mu, nu = tensor.shape
    step = 2
    return pl.pallas_call(
        mask_kernel,
        out_shape=jax.ShapeDtypeStruct((COLS, aux, mu // COLS, nu), jnp.bfloat16),
        grid=(aux // step,),
        in_specs=[
            pl.BlockSpec(memory_space=pltpu.SMEM),
            pl.BlockSpec((step, mu, nu), lambda p: (p, 0, 0)),
        ],
        out_specs=pl.BlockSpec((COLS, step, mu // COLS, nu), lambda p: (0, p, 0, 0)),
        compiler_params=pltpu.CompilerParams(vmem_limit_bytes=6 * MIB),
        name="masked_tensor",
        cost_estimate=pl.CostEstimate(flops=2 * tensor.size, bytes_accessed=4 * tensor.size, transcendentals=0),
    )(tile_mask, tensor)


def product_kernel(tensor_ref, coefs_ref, out_ref):
    rows = tensor_ref.shape[1]
    for c in range(COLS):
        product = jnp.dot(tensor_ref[c], coefs_ref[...], preferred_element_type=jnp.float32)
        largest = jnp.max(jnp.abs(product), axis=(0, 1), keepdims=True)
        power = jnp.ceil(jnp.log2(jnp.maximum(largest, 1e-30)))
        scaled = product * jnp.exp2(15.0 - power)
        out_ref[c, :rows, :] = scaled[:, :HALF].astype(out_ref.dtype)
        out_ref[c, rows:2 * rows, :] = scaled[:, HALF:].astype(out_ref.dtype)
        out_ref[c, 2 * rows:, :] = jnp.broadcast_to(power, (SCALE_ROWS, HALF)).astype(out_ref.dtype)


def product(masked, batch):
    rows = masked.shape[1]
    return pl.pallas_call(
        product_kernel,
        out_shape=jax.ShapeDtypeStruct((COLS, 2 * rows + SCALE_ROWS, HALF), jnp.float32),
        in_specs=[pl.BlockSpec(memory_space=pltpu.VMEM)] * 2,
        out_specs=pl.BlockSpec(memory_space=pltpu.VMEM),
        compiler_params=pltpu.CompilerParams(vmem_limit_bytes=10 * MIB),
        name="product",
        cost_estimate=pl.CostEstimate(flops=2 * masked.size * BATCH, bytes_accessed=2 * masked.size, transcendentals=0),
    )(masked, batch)


def total_kernel(got_ref, out_ref):
    aux, mu, _ = out_ref.shape
    rows = aux * mu
    low = jnp.zeros((rows, HALF), jnp.float32)
    high = jnp.zeros((rows, HALF), jnp.float32)
    for c in range(COLS):
        power = got_ref[c, 2 * rows:2 * rows + SCALE_ROWS, :].astype(jnp.float32)[:1]
        scale = jnp.exp2(power - 15.0)
        low += got_ref[c, :rows, :].astype(jnp.float32) * scale
        high += got_ref[c, rows:2 * rows, :].astype(jnp.float32) * scale
    out_ref[:, :, :HALF] = low.astype(out_ref.dtype).reshape(aux, mu, HALF)
    out_ref[:, :, HALF:] = high.astype(out_ref.dtype).reshape(aux, mu, HALF)


def total(got, aux, mu):
    return pl.pallas_call(
        total_kernel,
        out_shape=jax.ShapeDtypeStruct((aux, mu, BATCH), jnp.bfloat16),
        in_specs=[pl.BlockSpec(memory_space=pltpu.VMEM)],
        out_specs=pl.BlockSpec(memory_space=pltpu.VMEM),
        compiler_params=pltpu.CompilerParams(vmem_limit_bytes=4 * MIB),
        name="total",
    )(got)


def on_device(tensor, coefs, tile_mask, coef_mask, batch_start):
    aux, mu, nu = tensor.shape
    fetched = lax.ppermute(coefs, ("lp", "lb", "zh", "x"), fetch_pairs())
    batch = lax.all_to_all(spread_batch(fetched, coef_mask, batch_start), ("lb", "x"), 0, 0, tiled=True)
    masked = masked_tensor(tensor, tile_mask).reshape(COLS, aux * mu // COLS, nu)
    sent = product(masked, batch.reshape(nu, BATCH)).astype(jnp.float16)
    got = lax.all_to_all(sent, "col", 0, 0, tiled=True).astype(jnp.float32)
    return total(got, aux, mu // COLS)


def solution(mesh):
    fine = Mesh(mesh.devices.reshape(4, 2, 2, 4, 8), ("lp", "lb", "zh", "x", "col"))
    aux = ("lp", "lb", "zh", "x")
    in_specs = (P(aux, None, "col"), P(("col", "lp", "lb"), None), P(), P(), P())
    out_specs = P(aux, "col", None)
    return jax.shard_map(on_device, mesh=fine, in_specs=in_specs, out_specs=out_specs, check_vma=False)
```

```python
import jax
import jax.numpy as jnp
from jax import lax
from jax.experimental import pallas as pl
from jax.experimental.pallas import tpu as pltpu
from jax.sharding import Mesh, PartitionSpec as P

TILE = 64
BATCH = 256
HALF = 128
LAYERS = 8
COLS = 8
SCALE_ROWS = 8
MIB = 1 << 20
FETCH_OFFSETS = ((-3, -2, -1, 0), (3, 2, 1, 0), (0, -2, -1, -3), (0, 2, 1, 3))
SLOT_BLOCKS = tuple(
    FETCH_OFFSETS[2 * odd] + tuple(1 + offset for offset in FETCH_OFFSETS[2 * odd + 1]) for odd in range(2)
)


def fetch_pairs():
    pairs = []
    for z in range(16):
        for x in range(4):
            source = (z + FETCH_OFFSETS[z % 4][x]) % 16
            pairs.append(((source % 8) * 8 + (source // 8) * 4 + x, (z % 8) * 8 + (z // 8) * 4 + x))
    return pairs


def block_of(slot):
    pair = lax.axis_index("lp")
    offset = jnp.where(lax.rem(pair, 2) == 0, jnp.int32(SLOT_BLOCKS[0][slot]), jnp.int32(SLOT_BLOCKS[1][slot]))
    return lax.rem(2 * pair + LAYERS + offset, LAYERS)


def keep_kernel(mask_ref, out_ref):
    tiles, width = out_ref.shape
    slot = 4 * lax.axis_index("lb") + lax.axis_index("x")
    block = block_of(0)
    for at in range(1, LAYERS):
        block = jnp.where(slot == at, block_of(at), block)
    first = (lax.axis_index("col") * LAYERS + block) * tiles
    lane_tile = lax.broadcasted_iota(jnp.int32, (1, width), 1) // TILE
    for t in range(tiles):
        keep = jnp.zeros((1, width), jnp.int32)
        for j in range(width // TILE):
            keep = jnp.where(lane_tile == j, mask_ref[j, first + t], keep)
        out_ref[t:t + 1, :] = keep


def keep_rows(coef_mask, tiles):
    return pl.pallas_call(
        keep_kernel,
        out_shape=jax.ShapeDtypeStruct((tiles, coef_mask.shape[1] * TILE), jnp.int32),
        in_specs=[pl.BlockSpec(memory_space=pltpu.SMEM)],
        out_specs=pl.BlockSpec(memory_space=pltpu.VMEM),
        compiler_params=pltpu.CompilerParams(vmem_limit_bytes=MIB),
        name="keep_rows",
    )(coef_mask.T)


def spread_kernel(start_ref, keep_ref, coefs_ref, out_ref, batch_ref, sems):
    width = coefs_ref.shape[1]
    turn = lax.rem(width - start_ref[0], width)
    for t in range(keep_ref.shape[0]):
        rows = slice(t * TILE, (t + 1) * TILE)
        kept = jnp.where(keep_ref[t:t + 1, :] > 0, coefs_ref[rows, :].astype(jnp.float32), 0.0)
        batch_ref[rows, :] = pltpu.roll(kept, turn, 1)[:, :BATCH].astype(batch_ref.dtype)
    copies = [pltpu.make_async_copy(batch_ref, out_ref.at[s], sems.at[s]) for s in range(LAYERS)]
    for copy in copies:
        copy.start()
    for copy in copies:
        copy.wait()


def spread_batch(fetched, keep, batch_start):
    rows = fetched.shape[0]
    return pl.pallas_call(
        spread_kernel,
        out_shape=jax.ShapeDtypeStruct((LAYERS, rows, BATCH), jnp.bfloat16),
        in_specs=[
            pl.BlockSpec(memory_space=pltpu.SMEM),
            pl.BlockSpec(memory_space=pltpu.VMEM),
            pl.BlockSpec(memory_space=pltpu.VMEM),
        ],
        out_specs=pl.BlockSpec(memory_space=pl.ANY),
        scratch_shapes=[pltpu.VMEM((rows, BATCH), jnp.bfloat16), pltpu.SemaphoreType.DMA((LAYERS,))],
        compiler_params=pltpu.CompilerParams(vmem_limit_bytes=2 * MIB),
        name="spread_batch",
    )(batch_start, keep, fetched)


def mask_kernel(mask_ref, tensor_ref, out_ref):
    layer = 2 * lax.axis_index("lp") + lax.axis_index("lb")
    col = lax.axis_index("col")
    mu_dev = tensor_ref.shape[1] // COLS
    left = lax.broadcasted_iota(jnp.int32, (1, 1, HALF), 2) < TILE
    for s in range(LAYERS):
        block = block_of(s)
        first = col * (2 * LAYERS) + 2 * block
        lanes = pl.ds(pl.multiple_of(block * HALF, HALF), HALF)
        for c in range(COLS):
            keep = jnp.where(left, mask_ref[layer, c, first], mask_ref[layer, c, first + 1])
            part = tensor_ref[:, c * mu_dev:(c + 1) * mu_dev, lanes]
            out_ref[c, :, :, s * HALF:(s + 1) * HALF] = jnp.where(keep > 0, part, jnp.zeros_like(part))


def masked_tensor(tensor, tile_mask):
    aux, mu, nu = tensor.shape
    step = 2
    return pl.pallas_call(
        mask_kernel,
        out_shape=jax.ShapeDtypeStruct((COLS, aux, mu // COLS, nu), jnp.bfloat16),
        grid=(aux // step,),
        in_specs=[
            pl.BlockSpec(memory_space=pltpu.SMEM),
            pl.BlockSpec((step, mu, nu), lambda p: (p, 0, 0)),
        ],
        out_specs=pl.BlockSpec((COLS, step, mu // COLS, nu), lambda p: (0, p, 0, 0)),
        compiler_params=pltpu.CompilerParams(vmem_limit_bytes=6 * MIB),
        name="masked_tensor",
        cost_estimate=pl.CostEstimate(flops=2 * tensor.size, bytes_accessed=4 * tensor.size, transcendentals=0),
    )(tile_mask, tensor)


def product_kernel(tensor_ref, coefs_ref, out_ref):
    rows = tensor_ref.shape[1]
    for c in range(COLS):
        product = jnp.dot(tensor_ref[c], coefs_ref[...], preferred_element_type=jnp.float32)
        largest = jnp.max(jnp.abs(product), axis=(0, 1), keepdims=True)
        power = jnp.ceil(jnp.log2(jnp.maximum(largest, 1e-30)))
        scaled = product * jnp.exp2(15.0 - power)
        out_ref[c, :rows, :] = scaled[:, :HALF].astype(out_ref.dtype)
        out_ref[c, rows:2 * rows, :] = scaled[:, HALF:].astype(out_ref.dtype)
        out_ref[c, 2 * rows:, :] = jnp.broadcast_to(power, (SCALE_ROWS, HALF)).astype(out_ref.dtype)


def product(masked, batch):
    rows = masked.shape[1]
    return pl.pallas_call(
        product_kernel,
        out_shape=jax.ShapeDtypeStruct((COLS, 2 * rows + SCALE_ROWS, HALF), jnp.float32),
        in_specs=[pl.BlockSpec(memory_space=pltpu.VMEM)] * 2,
        out_specs=pl.BlockSpec(memory_space=pltpu.VMEM),
        compiler_params=pltpu.CompilerParams(vmem_limit_bytes=10 * MIB),
        name="product",
        cost_estimate=pl.CostEstimate(flops=2 * masked.size * BATCH, bytes_accessed=2 * masked.size, transcendentals=0),
    )(masked, batch)


def total_kernel(got_ref, out_ref):
    aux, mu, _ = out_ref.shape
    rows = aux * mu
    low = jnp.zeros((rows, HALF), jnp.float32)
    high = jnp.zeros((rows, HALF), jnp.float32)
    for c in range(COLS):
        power = got_ref[c, 2 * rows:2 * rows + SCALE_ROWS, :].astype(jnp.float32)[:1]
        scale = jnp.exp2(power - 15.0)
        low += got_ref[c, :rows, :].astype(jnp.float32) * scale
        high += got_ref[c, rows:2 * rows, :].astype(jnp.float32) * scale
    out_ref[:, :, :HALF] = low.astype(out_ref.dtype).reshape(aux, mu, HALF)
    out_ref[:, :, HALF:] = high.astype(out_ref.dtype).reshape(aux, mu, HALF)


def total(got, aux, mu):
    return pl.pallas_call(
        total_kernel,
        out_shape=jax.ShapeDtypeStruct((aux, mu, BATCH), jnp.bfloat16),
        in_specs=[pl.BlockSpec(memory_space=pltpu.VMEM)],
        out_specs=pl.BlockSpec(memory_space=pltpu.VMEM),
        compiler_params=pltpu.CompilerParams(vmem_limit_bytes=4 * MIB),
        name="total",
    )(got)


def on_device(tensor, coefs, tile_mask, coef_mask, batch_start):
    aux, mu, nu = tensor.shape
    fetched = lax.ppermute(coefs, ("lp", "lb", "zh", "x"), fetch_pairs())
    keep = keep_rows(coef_mask, coefs.shape[0] // TILE)
    batch = lax.all_to_all(spread_batch(fetched, keep, batch_start), ("lb", "x"), 0, 0, tiled=True)
    masked = masked_tensor(tensor, tile_mask).reshape(COLS, aux * mu // COLS, nu)
    sent = product(masked, batch.reshape(nu, BATCH)).astype(jnp.float16)
    got = lax.all_to_all(sent, "col", 0, 0, tiled=True).astype(jnp.float32)
    return total(got, aux, mu // COLS)


def solution(mesh):
    fine = Mesh(mesh.devices.reshape(4, 2, 2, 4, 8), ("lp", "lb", "zh", "x", "col"))
    aux = ("lp", "lb", "zh", "x")
    in_specs = (P(aux, None, "col"), P(("col", "lp", "lb"), None), P(), P(), P())
    out_specs = P(aux, "col", None)
    return jax.shard_map(on_device, mesh=fine, in_specs=in_specs, out_specs=out_specs, check_vma=False)
```

```python
import jax
import jax.numpy as jnp
from jax import lax
from jax.experimental import pallas as pl
from jax.experimental.pallas import tpu as pltpu
from jax.sharding import Mesh, PartitionSpec as P

TILE = 64
BATCH = 256
HALF = 128
LAYERS = 8
COLS = 8
CORES = 2
RINGS = COLS // CORES
SCALE_ROWS = 8
MIB = 1 << 20
FETCH_OFFSETS = ((-3, -2, -1, 0), (3, 2, 1, 0), (0, -2, -1, -3), (0, 2, 1, 3))
SLOT_BLOCKS = tuple(
    FETCH_OFFSETS[2 * odd] + tuple(1 + offset for offset in FETCH_OFFSETS[2 * odd + 1]) for odd in range(2)
)


def fetch_pairs():
    pairs = []
    for z in range(16):
        for x in range(4):
            source = (z + FETCH_OFFSETS[z % 4][x]) % 16
            pairs.append(((source % 8) * 8 + (source // 8) * 4 + x, (z % 8) * 8 + (z // 8) * 4 + x))
    return pairs


def block_of(slot):
    pair = lax.axis_index("lp")
    offset = jnp.where(lax.rem(pair, 2) == 0, jnp.int32(SLOT_BLOCKS[0][slot]), jnp.int32(SLOT_BLOCKS[1][slot]))
    return lax.rem(2 * pair + LAYERS + offset, LAYERS)


def col_index():
    return CORES * lax.axis_index("y") + lax.axis_index("core")


def keep_kernel(mask_ref, out_ref):
    tiles, width = out_ref.shape
    slot = 4 * lax.axis_index("lb") + lax.axis_index("x")
    block = block_of(0)
    for at in range(1, LAYERS):
        block = jnp.where(slot == at, block_of(at), block)
    first = (col_index() * LAYERS + block) * tiles
    lane_tile = lax.broadcasted_iota(jnp.int32, (1, width), 1) // TILE
    for t in range(tiles):
        keep = jnp.zeros((1, width), jnp.int32)
        for j in range(width // TILE):
            keep = jnp.where(lane_tile == j, mask_ref[j, first + t], keep)
        out_ref[t:t + 1, :] = keep


def keep_rows(coef_mask, tiles):
    return pl.pallas_call(
        keep_kernel,
        out_shape=jax.ShapeDtypeStruct((tiles, coef_mask.shape[1] * TILE), jnp.int32),
        in_specs=[pl.BlockSpec(memory_space=pltpu.SMEM)],
        out_specs=pl.BlockSpec(memory_space=pltpu.VMEM),
        compiler_params=pltpu.CompilerParams(vmem_limit_bytes=MIB),
        name="keep_rows",
    )(coef_mask.T)


def spread_kernel(start_ref, keep_ref, coefs_ref, out_ref, batch_ref, sems):
    width = coefs_ref.shape[1]
    turn = lax.rem(width - start_ref[0], width)
    for t in range(keep_ref.shape[0]):
        rows = slice(t * TILE, (t + 1) * TILE)
        kept = jnp.where(keep_ref[t:t + 1, :] > 0, coefs_ref[rows, :].astype(jnp.float32), 0.0)
        batch_ref[rows, :] = pltpu.roll(kept, turn, 1)[:, :BATCH].astype(batch_ref.dtype)
    copies = [pltpu.make_async_copy(batch_ref, out_ref.at[s], sems.at[s]) for s in range(LAYERS)]
    for copy in copies:
        copy.start()
    for copy in copies:
        copy.wait()


def spread_batch(fetched, keep, batch_start):
    rows = fetched.shape[0]
    return pl.pallas_call(
        spread_kernel,
        out_shape=jax.ShapeDtypeStruct((LAYERS, rows, BATCH), jnp.bfloat16),
        in_specs=[
            pl.BlockSpec(memory_space=pltpu.SMEM),
            pl.BlockSpec(memory_space=pltpu.VMEM),
            pl.BlockSpec(memory_space=pltpu.VMEM),
        ],
        out_specs=pl.BlockSpec(memory_space=pl.ANY),
        scratch_shapes=[pltpu.VMEM((rows, BATCH), jnp.bfloat16), pltpu.SemaphoreType.DMA((LAYERS,))],
        compiler_params=pltpu.CompilerParams(vmem_limit_bytes=2 * MIB),
        name="spread_batch",
    )(batch_start, keep, fetched)


def mask_kernel(mask_ref, tensor_ref, out_ref):
    layer = 2 * lax.axis_index("lp") + lax.axis_index("lb")
    col = col_index()
    core = lax.axis_index("core")
    mu_dev = tensor_ref.shape[1] // COLS
    left = lax.broadcasted_iota(jnp.int32, (1, 1, HALF), 2) < TILE
    for s in range(LAYERS):
        block = block_of(s)
        first = col * (2 * LAYERS) + 2 * block
        lanes = pl.ds(pl.multiple_of(block * HALF, HALF), HALF)
        for c in range(COLS):
            keep = jnp.where(left, mask_ref[layer, c, first], mask_ref[layer, c, first + 1])
            part = tensor_ref[:, c * mu_dev:(c + 1) * mu_dev, lanes]
            place = c // CORES + jnp.where(core == c % CORES, 0, RINGS)
            out_ref[place, :, :, s * HALF:(s + 1) * HALF] = jnp.where(keep > 0, part, jnp.zeros_like(part))


def masked_tensor(tensor, tile_mask):
    aux, mu, nu = tensor.shape
    return pl.pallas_call(
        mask_kernel,
        out_shape=jax.ShapeDtypeStruct((COLS, aux, mu // COLS, nu), jnp.bfloat16),
        in_specs=[
            pl.BlockSpec(memory_space=pltpu.SMEM),
            pl.BlockSpec(memory_space=pltpu.VMEM),
        ],
        out_specs=pl.BlockSpec(memory_space=pltpu.VMEM),
        compiler_params=pltpu.CompilerParams(vmem_limit_bytes=6 * MIB),
        name="masked_tensor",
        cost_estimate=pl.CostEstimate(flops=2 * tensor.size, bytes_accessed=4 * tensor.size, transcendentals=0),
    )(tile_mask, tensor)


def put_scaled(out_ref, at, values):
    rows = values.shape[0]
    largest = jnp.max(jnp.abs(values), axis=(0, 1), keepdims=True)
    power = jnp.ceil(jnp.log2(jnp.maximum(largest, 1e-30)))
    scaled = values * jnp.exp2(15.0 - power)
    out_ref[at, :rows, :] = scaled[:, :HALF]
    out_ref[at, rows:2 * rows, :] = scaled[:, HALF:]
    out_ref[at, 2 * rows:, :] = jnp.broadcast_to(power, (SCALE_ROWS, HALF))


def product_kernel(tensor_ref, coefs_ref, mine_ref, theirs_ref):
    rows = tensor_ref.shape[1]
    lhs = tensor_ref[...].reshape(COLS * rows, tensor_ref.shape[2])
    products = jnp.dot(lhs, coefs_ref[...], preferred_element_type=jnp.float32)
    for y in range(RINGS):
        mine_ref[y] = products[y * rows:(y + 1) * rows]
        at = (RINGS + y) * rows
        put_scaled(theirs_ref, y, products[at:at + rows])


def product(masked, batch):
    rows = masked.shape[1]
    return pl.pallas_call(
        product_kernel,
        out_shape=[
            jax.ShapeDtypeStruct((RINGS, rows, BATCH), jnp.float32),
            jax.ShapeDtypeStruct((RINGS, 2 * rows + SCALE_ROWS, HALF), jnp.float32),
        ],
        in_specs=[pl.BlockSpec(memory_space=pltpu.VMEM)] * 2,
        out_specs=[pl.BlockSpec(memory_space=pltpu.VMEM)] * 2,
        compiler_params=pltpu.CompilerParams(vmem_limit_bytes=10 * MIB),
        name="product",
        cost_estimate=pl.CostEstimate(flops=2 * masked.size * BATCH, bytes_accessed=2 * masked.size, transcendentals=0),
    )(masked, batch)


def chip_kernel(mine_ref, both_ref, out_ref):
    rows = mine_ref.shape[1]
    other = 1 - lax.axis_index("core")
    for y in range(RINGS):
        scale = jnp.exp2(both_ref[other, y, 2 * rows:2 * rows + 1, :] - 15.0)
        low = mine_ref[y, :, :HALF] + both_ref[other, y, :rows, :] * scale
        high = mine_ref[y, :, HALF:] + both_ref[other, y, rows:2 * rows, :] * scale
        put_scaled(out_ref, y, jnp.concatenate([low, high], axis=1))


def chip_sum(mine, both):
    return pl.pallas_call(
        chip_kernel,
        out_shape=jax.ShapeDtypeStruct(both.shape[1:], jnp.float32),
        in_specs=[pl.BlockSpec(memory_space=pltpu.VMEM)] * 2,
        out_specs=pl.BlockSpec(memory_space=pltpu.VMEM),
        compiler_params=pltpu.CompilerParams(vmem_limit_bytes=4 * MIB),
        name="chip_sum",
    )(mine, both)


def total_kernel(got_ref, out_ref):
    aux, mu, _ = out_ref.shape
    rows = aux * mu
    low = jnp.zeros((rows, HALF), jnp.float32)
    high = jnp.zeros((rows, HALF), jnp.float32)
    for y in range(RINGS):
        scale = jnp.exp2(got_ref[y, 2 * rows:2 * rows + 1, :] - 15.0)
        low += got_ref[y, :rows, :] * scale
        high += got_ref[y, rows:2 * rows, :] * scale
    out_ref[:, :, :HALF] = low.astype(out_ref.dtype).reshape(aux, mu, HALF)
    out_ref[:, :, HALF:] = high.astype(out_ref.dtype).reshape(aux, mu, HALF)


def total(got, aux, mu):
    return pl.pallas_call(
        total_kernel,
        out_shape=jax.ShapeDtypeStruct((aux, mu, BATCH), jnp.bfloat16),
        in_specs=[pl.BlockSpec(memory_space=pltpu.VMEM)],
        out_specs=pl.BlockSpec(memory_space=pltpu.VMEM),
        compiler_params=pltpu.CompilerParams(vmem_limit_bytes=4 * MIB),
        name="total",
    )(got)


def on_device(tensor, coefs, tile_mask, coef_mask, batch_start):
    aux, mu, nu = tensor.shape
    fetched = lax.ppermute(coefs, ("lp", "lb", "zh", "x"), fetch_pairs())
    keep = keep_rows(coef_mask, coefs.shape[0] // TILE)
    batch = lax.all_to_all(spread_batch(fetched, keep, batch_start), ("lb", "x"), 0, 0, tiled=True)
    masked = masked_tensor(tensor, tile_mask).reshape(COLS, aux * mu // COLS, nu)
    mine, theirs = product(masked, batch.reshape(nu, BATCH))
    both = lax.all_gather(theirs.astype(jnp.float16), "core").astype(jnp.float32)
    sent = chip_sum(mine, both).astype(jnp.float16)
    got = lax.all_to_all(sent, "y", 0, 0, tiled=True).astype(jnp.float32)
    return total(got, aux, mu // COLS)


def solution(mesh):
    fine = Mesh(mesh.devices.reshape(4, 2, 2, 4, 4, 2), ("lp", "lb", "zh", "x", "y", "core"))
    aux = ("lp", "lb", "zh", "x")
    in_specs = (P(aux, None, ("y", "core")), P(("y", "core", "lp", "lb"), None), P(), P(), P())
    out_specs = P(aux, ("y", "core"), None)
    return jax.shard_map(on_device, mesh=fine, in_specs=in_specs, out_specs=out_specs, check_vma=False)
```

```python
import jax
import jax.numpy as jnp
from jax import lax
from jax.experimental import pallas as pl
from jax.experimental.pallas import tpu as pltpu
from jax.sharding import Mesh, PartitionSpec as P

TILE = 64
BATCH = 256
HALF = 128
LAYERS = 8
COLS = 8
CORES = 2
RINGS = COLS // CORES
SCALE_ROWS = 8
MIB = 1 << 20
FETCH_OFFSETS = ((-2, -3, 0, -1), (2, 3, 0, 1), (-2, 0, -3, -1), (2, 0, 3, 1))
SLOT_BLOCKS = tuple(
    FETCH_OFFSETS[2 * odd] + tuple(1 + offset for offset in FETCH_OFFSETS[2 * odd + 1]) for odd in range(2)
)


def fetch_pairs():
    pairs = []
    for z in range(16):
        for x in range(4):
            source = (z + FETCH_OFFSETS[z % 4][x]) % 16
            pairs.append(((source % 8) * 8 + (source // 8) * 4 + x, (z % 8) * 8 + (z // 8) * 4 + x))
    return pairs


def block_of(slot):
    pair = lax.axis_index("lp")
    offset = jnp.where(lax.rem(pair, 2) == 0, jnp.int32(SLOT_BLOCKS[0][slot]), jnp.int32(SLOT_BLOCKS[1][slot]))
    return lax.rem(2 * pair + LAYERS + offset, LAYERS)


def col_index():
    return CORES * lax.axis_index("y") + lax.axis_index("core")


def keep_kernel(mask_ref, out_ref):
    tiles, width = out_ref.shape
    slot = 4 * lax.axis_index("lb") + lax.axis_index("x")
    block = block_of(0)
    for at in range(1, LAYERS):
        block = jnp.where(slot == at, block_of(at), block)
    first = (col_index() * LAYERS + block) * tiles
    lane_tile = lax.broadcasted_iota(jnp.int32, (1, width), 1) // TILE
    for t in range(tiles):
        keep = jnp.zeros((1, width), jnp.int32)
        for j in range(width // TILE):
            keep = jnp.where(lane_tile == j, mask_ref[j, first + t], keep)
        out_ref[t:t + 1, :] = keep


def keep_rows(coef_mask, tiles):
    return pl.pallas_call(
        keep_kernel,
        out_shape=jax.ShapeDtypeStruct((tiles, coef_mask.shape[1] * TILE), jnp.int32),
        in_specs=[pl.BlockSpec(memory_space=pltpu.SMEM)],
        out_specs=pl.BlockSpec(memory_space=pltpu.VMEM),
        compiler_params=pltpu.CompilerParams(vmem_limit_bytes=MIB),
        name="keep_rows",
    )(coef_mask.T)


def spread_kernel(start_ref, keep_ref, coefs_ref, out_ref, batch_ref, sems):
    width = coefs_ref.shape[1]
    turn = lax.rem(width - start_ref[0], width)
    for t in range(keep_ref.shape[0]):
        rows = slice(t * TILE, (t + 1) * TILE)
        kept = jnp.where(keep_ref[t:t + 1, :] > 0, coefs_ref[rows, :].astype(jnp.float32), 0.0)
        batch_ref[rows, :] = pltpu.roll(kept, turn, 1)[:, :BATCH].astype(batch_ref.dtype)
    copies = [pltpu.make_async_copy(batch_ref, out_ref.at[s], sems.at[s]) for s in range(LAYERS)]
    for copy in copies:
        copy.start()
    for copy in copies:
        copy.wait()


def spread_batch(fetched, keep, batch_start):
    rows = fetched.shape[0]
    return pl.pallas_call(
        spread_kernel,
        out_shape=jax.ShapeDtypeStruct((LAYERS, rows, BATCH), jnp.bfloat16),
        in_specs=[
            pl.BlockSpec(memory_space=pltpu.SMEM),
            pl.BlockSpec(memory_space=pltpu.VMEM),
            pl.BlockSpec(memory_space=pltpu.VMEM),
        ],
        out_specs=pl.BlockSpec(memory_space=pl.ANY),
        scratch_shapes=[pltpu.VMEM((rows, BATCH), jnp.bfloat16), pltpu.SemaphoreType.DMA((LAYERS,))],
        compiler_params=pltpu.CompilerParams(vmem_limit_bytes=2 * MIB),
        name="spread_batch",
    )(batch_start, keep, fetched)


def mask_kernel(mask_ref, tensor_ref, out_ref):
    layer = 2 * lax.axis_index("lp") + lax.axis_index("lb")
    col = col_index()
    core = lax.axis_index("core")
    mu_dev = tensor_ref.shape[1] // COLS
    left = lax.broadcasted_iota(jnp.int32, (1, 1, HALF), 2) < TILE
    for s in range(LAYERS):
        block = block_of(s)
        first = col * (2 * LAYERS) + 2 * block
        lanes = pl.ds(pl.multiple_of(block * HALF, HALF), HALF)
        for c in range(COLS):
            keep = jnp.where(left, mask_ref[layer, c, first], mask_ref[layer, c, first + 1])
            part = tensor_ref[:, c * mu_dev:(c + 1) * mu_dev, lanes]
            place = c // CORES + jnp.where(core == c % CORES, 0, RINGS)
            out_ref[place, :, :, s * HALF:(s + 1) * HALF] = jnp.where(keep > 0, part, jnp.zeros_like(part))


def masked_tensor(tensor, tile_mask):
    aux, mu, nu = tensor.shape
    return pl.pallas_call(
        mask_kernel,
        out_shape=jax.ShapeDtypeStruct((COLS, aux, mu // COLS, nu), jnp.bfloat16),
        in_specs=[
            pl.BlockSpec(memory_space=pltpu.SMEM),
            pl.BlockSpec(memory_space=pltpu.VMEM),
        ],
        out_specs=pl.BlockSpec(memory_space=pltpu.VMEM),
        compiler_params=pltpu.CompilerParams(vmem_limit_bytes=6 * MIB),
        name="masked_tensor",
        cost_estimate=pl.CostEstimate(flops=2 * tensor.size, bytes_accessed=4 * tensor.size, transcendentals=0),
    )(tile_mask, tensor)


def put_scaled(out_ref, at, values):
    rows = values.shape[0]
    largest = jnp.max(jnp.abs(values), axis=(0, 1), keepdims=True)
    power = jnp.ceil(jnp.log2(jnp.maximum(largest, 1e-30)))
    scaled = values * jnp.exp2(15.0 - power)
    out_ref[at, :rows, :] = scaled[:, :HALF]
    out_ref[at, rows:2 * rows, :] = scaled[:, HALF:]
    out_ref[at, 2 * rows:, :] = jnp.broadcast_to(power, (SCALE_ROWS, HALF))


def product_kernel(tensor_ref, coefs_ref, mine_ref, theirs_ref):
    rows = tensor_ref.shape[1]
    lhs = tensor_ref[...].reshape(COLS * rows, tensor_ref.shape[2])
    products = jnp.dot(lhs, coefs_ref[...], preferred_element_type=jnp.float32)
    for y in range(RINGS):
        mine_ref[y] = products[y * rows:(y + 1) * rows]
        at = (RINGS + y) * rows
        put_scaled(theirs_ref, y, products[at:at + rows])


def product(masked, batch):
    rows = masked.shape[1]
    return pl.pallas_call(
        product_kernel,
        out_shape=[
            jax.ShapeDtypeStruct((RINGS, rows, BATCH), jnp.float32),
            jax.ShapeDtypeStruct((RINGS, 2 * rows + SCALE_ROWS, HALF), jnp.float32),
        ],
        in_specs=[pl.BlockSpec(memory_space=pltpu.VMEM)] * 2,
        out_specs=[pl.BlockSpec(memory_space=pltpu.VMEM)] * 2,
        compiler_params=pltpu.CompilerParams(vmem_limit_bytes=10 * MIB),
        name="product",
        cost_estimate=pl.CostEstimate(flops=2 * masked.size * BATCH, bytes_accessed=2 * masked.size, transcendentals=0),
    )(masked, batch)


def chip_kernel(mine_ref, both_ref, out_ref):
    rows = mine_ref.shape[1]
    other = 1 - lax.axis_index("core")
    for y in range(RINGS):
        scale = jnp.exp2(both_ref[other, y, 2 * rows:2 * rows + 1, :] - 15.0)
        low = mine_ref[y, :, :HALF] + both_ref[other, y, :rows, :] * scale
        high = mine_ref[y, :, HALF:] + both_ref[other, y, rows:2 * rows, :] * scale
        put_scaled(out_ref, y, jnp.concatenate([low, high], axis=1))


def chip_sum(mine, both):
    return pl.pallas_call(
        chip_kernel,
        out_shape=jax.ShapeDtypeStruct(both.shape[1:], jnp.float32),
        in_specs=[pl.BlockSpec(memory_space=pltpu.VMEM)] * 2,
        out_specs=pl.BlockSpec(memory_space=pltpu.VMEM),
        compiler_params=pltpu.CompilerParams(vmem_limit_bytes=4 * MIB),
        name="chip_sum",
    )(mine, both)


def total_kernel(got_ref, out_ref):
    aux, mu, _ = out_ref.shape
    rows = aux * mu
    low = jnp.zeros((rows, HALF), jnp.float32)
    high = jnp.zeros((rows, HALF), jnp.float32)
    for y in range(RINGS):
        scale = jnp.exp2(got_ref[y, 2 * rows:2 * rows + 1, :] - 15.0)
        low += got_ref[y, :rows, :] * scale
        high += got_ref[y, rows:2 * rows, :] * scale
    out_ref[:, :, :HALF] = low.astype(out_ref.dtype).reshape(aux, mu, HALF)
    out_ref[:, :, HALF:] = high.astype(out_ref.dtype).reshape(aux, mu, HALF)


def total(got, aux, mu):
    return pl.pallas_call(
        total_kernel,
        out_shape=jax.ShapeDtypeStruct((aux, mu, BATCH), jnp.bfloat16),
        in_specs=[pl.BlockSpec(memory_space=pltpu.VMEM)],
        out_specs=pl.BlockSpec(memory_space=pltpu.VMEM),
        compiler_params=pltpu.CompilerParams(vmem_limit_bytes=4 * MIB),
        name="total",
    )(got)


def on_device(tensor, coefs, tile_mask, coef_mask, batch_start):
    aux, mu, nu = tensor.shape
    fetched = lax.ppermute(coefs, ("lp", "lb", "zh", "x"), fetch_pairs())
    keep = keep_rows(coef_mask, coefs.shape[0] // TILE)
    batch = lax.all_to_all(spread_batch(fetched, keep, batch_start), ("lb", "x"), 0, 0, tiled=True)
    masked = masked_tensor(tensor, tile_mask).reshape(COLS, aux * mu // COLS, nu)
    mine, theirs = product(masked, batch.reshape(nu, BATCH))
    both = lax.all_gather(theirs.astype(jnp.float16), "core").astype(jnp.float32)
    sent = chip_sum(mine, both).astype(jnp.float16)
    got = lax.all_to_all(sent, "y", 0, 0, tiled=True).astype(jnp.float32)
    return total(got, aux, mu // COLS)


def solution(mesh):
    fine = Mesh(mesh.devices.reshape(4, 2, 2, 4, 4, 2), ("lp", "lb", "zh", "x", "y", "core"))
    aux = ("lp", "lb", "zh", "x")
    in_specs = (P(aux, None, ("y", "core")), P(("y", "core", "lp", "lb"), None), P(), P(), P())
    out_specs = P(aux, ("y", "core"), None)
    return jax.shard_map(on_device, mesh=fine, in_specs=in_specs, out_specs=out_specs, check_vma=False)
```
